32 devices in a mesh: group: 2 (over y), replica: 4 (over z), tensor: 2 (over x), sub: 2 (over core).
Axes of the slice: x: 2, y: 2, z: 4, core: 2. Of those that a mesh axis runs over, the one named last changes fastest.
Arguments:
- queries: bfloat16 [2048, 4096], P(('group', 'replica'), ('tensor', 'sub')), parts along dimension 0, may hold values from -20 to 20
- incoming_keys: bfloat16 [2048, 512], P(('group', 'replica'), 'tensor'), parts along dimension 0, may hold values from -4 to 4
- incoming_values: bfloat16 [2048, 512], P(('group', 'replica'), 'tensor'), parts along dimension 0, may hold values from -6 to 6
- cached_key_rows: bfloat16 [2048, 32, 512], P(('group', 'replica'), None, 'tensor'), parts along dimension 0, may hold values from -4 to 4
- cached_value_rows: bfloat16 [2048, 32, 512], P(('group', 'replica'), None, 'tensor'), parts along dimension 0, may hold values from -6 to 6
- cache_length: int32 [2048], P(('group', 'replica')), parts along dimension 0, may hold values from 1 to 32, as said below
- adapter_of_row: int32 [2048], P(('group', 'replica')), parts along dimension 0, may hold values from 0 to 15, as said below
- adapter_slot_table: int32 [32], P('group'), parts along dimension 0, may hold values from 0 to 15, as said below
- output_projection: bfloat16 [4096, 8192], P(('tensor', 'sub')), may hold values from -0.1875 to 0.1875
- adapter_down_weights: bfloat16 [16, 4096, 64], P('replica', ('tensor', 'sub')), may hold values from -0.1875 to 0.1875
- adapter_up_weights: bfloat16 [16, 64, 8192], P('replica', None, ('tensor', 'sub')), may hold values from -1.5 to 1.5
Outputs:
- projected: bfloat16 [2048, 8192], P(('group', 'replica'), ('tensor', 'sub')), parts along dimension 0
The draws below stay inside these ranges and needn't reach their ends.
There are 2 independent parts, one for each index of `group`. The reference program is written for one: setup_inputs(seed, part) draws one part's arguments, and reference() takes and returns one part's arrays. A program takes and returns all parts, laid end to end along the dimension named above; an argument that names none is the same for every part. Nothing has to cross between parts.
Inputs may be any that keep to these rules, and one draw needn't show every extreme that they name: A permutation: adapter a is stored in slot adapter_slot_table[a]. `adapter_of_row`: of the 256 rows of one replica, at most 64 use adapters stored on any one replica; in every draw some replica stores the adapters of exactly 64 rows of every replica. `cache_length`: some row has exactly 32.
All inputs are finite; a program needn't handle non-finite values.
Results may differ from the reference program's by a relative error of at most 0.0085.
Values may be sent and summed in bfloat16 or wider, within the bound.
A program may use at most 128 MiB of HBM per device.

```python
import jax
import jax.numpy as jnp
from jax import lax

MODEL_WIDTH = 8192
QUERY_HEADS = 32
KV_HEADS = 4
HEAD_WIDTH = 128
ADAPTER_RANK = 64
ROW_REP = 256
CTX = 32
ADP_REP = 4
CAP = 64
ROWS = 1024
ADAPTER_TOTAL = 16


def slot_table(key):
    return jax.random.permutation(jax.random.fold_in(key, 202), ADAPTER_TOTAL)


def draw_queries(key, part):
    key = jax.random.fold_in(key, 5)
    entries = jnp.clip(jax.random.normal(key, (ROWS, QUERY_HEADS * HEAD_WIDTH), jnp.float32), -6.0, 6.0)
    return entries.astype(jnp.bfloat16)


def draw_incoming_keys(key, part):
    key = jax.random.fold_in(key, 7)
    entries = jnp.clip(jax.random.normal(key, (ROWS, KV_HEADS * HEAD_WIDTH), jnp.float32), -4.0, 4.0)
    return entries.astype(jnp.bfloat16)


def draw_cached_key_rows(key, part):
    key = jax.random.fold_in(key, 13)
    entries = jnp.clip(jax.random.normal(key, (ROWS, CTX, KV_HEADS * HEAD_WIDTH), jnp.float32), -4.0, 4.0)
    return entries.astype(jnp.bfloat16)


def draw_cache_length(key, part):
    key = jax.random.fold_in(key, 17)
    drawn = jax.random.randint(jax.random.fold_in(key, 1), (ROWS,), 1, CTX + 1)
    longest = jax.random.randint(jax.random.fold_in(key, 2), (), 0, ROWS)
    return jnp.where(jnp.arange(ROWS) == longest, CTX, drawn).astype(jnp.int32)


def draw_adapter_slot_table(key, part):
    table = slot_table(key)
    return table.astype(jnp.int32)


def draw_adapter_of_row(key, part):
    table = slot_table(key)
    key = jax.random.fold_in(key, 23)
    inverse = jnp.argsort(table)
    replicas = ROWS // ROW_REP
    busiest = jax.random.randint(jax.random.fold_in(key, 1), (), 0, replicas)
    slot_ids = jnp.arange(replicas * CAP, dtype=jnp.int32)

    def one_block(block_key):
        ranking = jax.random.randint(jax.random.fold_in(block_key, 0), (replicas * CAP,), 0, 1 << 20)
        ranking = ranking * (replicas * CAP) + slot_ids
        ranking = jnp.where(slot_ids // CAP == busiest, slot_ids - replicas * CAP, ranking)
        picked = jnp.argsort(ranking)[:ROW_REP]
        picked = jax.random.permutation(jax.random.fold_in(block_key, 1), picked)
        return picked // CAP
    block_keys = jax.random.split(jax.random.fold_in(key, 2), replicas)
    owner_of_row = jax.vmap(one_block)(block_keys).reshape(ROWS)
    inner = jax.random.randint(jax.random.fold_in(key, 3), (ROWS,), 0, ADP_REP)
    return inverse[owner_of_row * ADP_REP + inner].astype(jnp.int32)


def block_scale(stream_key, dims, shards, low, high):
    def one(axis_at, blocks):
        steps = jax.random.uniform(jax.random.fold_in(jax.random.fold_in(stream_key, 6), axis_at), (blocks,), jnp.float32, low / len(shards), high / len(shards))
        return jnp.repeat(jnp.exp(steps), dims[axis_at] // blocks).reshape((-1,) + (1,) * (len(dims) - axis_at - 1))

    level = one(*shards[0])
    for cut in shards[1:]:
        level = level * one(*cut)
    return level


def normal_values(key, dims, spread, bound, cuts=(), held_as=jnp.bfloat16):
    loudness = block_scale(key, dims, cuts, -0.22, 0.18) if cuts else 1.0
    entries = jax.random.normal(key, dims, jnp.float32) * spread * loudness
    return jnp.minimum(jnp.maximum(entries, -bound), bound).astype(held_as)


def setup_inputs(seed: int = 0, part: int = 0) -> dict:
    arg_keys = jax.random.split(jax.random.key(seed), 12)
    part_keys = jax.random.split(jax.random.fold_in(arg_keys[11], part), 12)
    return {
        "queries": draw_queries(jax.random.fold_in(jax.random.fold_in(arg_keys[11], part), 71), part),
        "incoming_keys": draw_incoming_keys(jax.random.fold_in(jax.random.fold_in(arg_keys[11], part), 71), part),
        "incoming_values": normal_values(part_keys[2], (ROWS, KV_HEADS * HEAD_WIDTH), 1.0, 6.0, ((0, 4), (1, 2))),
        "cached_key_rows": draw_cached_key_rows(jax.random.fold_in(jax.random.fold_in(arg_keys[11], part), 71), part),
        "cached_value_rows": normal_values(part_keys[4], (ROWS, CTX, KV_HEADS * HEAD_WIDTH), 1.0, 6.0, ((0, 4), (2, 2))),
        "cache_length": draw_cache_length(jax.random.fold_in(jax.random.fold_in(arg_keys[11], part), 71), part),
        "adapter_of_row": draw_adapter_of_row(jax.random.fold_in(jax.random.fold_in(arg_keys[11], part), 71), part),
        "adapter_slot_table": draw_adapter_slot_table(jax.random.fold_in(jax.random.fold_in(arg_keys[11], part), 71), part),
        "output_projection": normal_values(arg_keys[8], (QUERY_HEADS * HEAD_WIDTH, MODEL_WIDTH), (QUERY_HEADS * HEAD_WIDTH // 4) ** -0.5, 0.1875, ((0, 4),)),
        "adapter_down_weights": normal_values(arg_keys[9], (ADAPTER_TOTAL, QUERY_HEADS * HEAD_WIDTH, ADAPTER_RANK), (QUERY_HEADS * HEAD_WIDTH // 4) ** -0.5, 0.1875, ((0, 4), (1, 4))),
        "adapter_up_weights": normal_values(arg_keys[10], (ADAPTER_TOTAL, ADAPTER_RANK, MODEL_WIDTH), (ADAPTER_RANK // 4) ** -0.5, 1.5, ((0, 4), (2, 4))),
    }


def attention_rows(queries, incoming_keys, incoming_values, cached_key_rows, cached_value_rows, cache_length):
    row_count = queries.shape[0]
    group_size = QUERY_HEADS // KV_HEADS
    query_all = queries.astype(jnp.float32).reshape(row_count, KV_HEADS, group_size, HEAD_WIDTH)
    keys_old = cached_key_rows.astype(jnp.float32).reshape(row_count, CTX, KV_HEADS, HEAD_WIDTH)
    values_old = cached_value_rows.astype(jnp.float32).reshape(row_count, CTX, KV_HEADS, HEAD_WIDTH)
    keys_now = incoming_keys.astype(jnp.float32).reshape(row_count, KV_HEADS, HEAD_WIDTH)
    values_now = incoming_values.astype(jnp.float32).reshape(row_count, KV_HEADS, HEAD_WIDTH)
    score_scale = HEAD_WIDTH ** -0.5
    scores = jnp.einsum("rkgd,rckd->rkgc", query_all, keys_old) * score_scale
    allowed = jnp.arange(CTX, dtype=jnp.int32)[None, :] < cache_length[:, None]
    scores = jnp.where(allowed[:, None, None, :], scores, -1e30)
    fresh = jnp.einsum("rkgd,rkd->rkg", query_all, keys_now) * score_scale
    highest = jnp.maximum(jnp.max(scores, axis=3), fresh)
    weights = jnp.exp(scores - highest[..., None])
    fresh_weight = jnp.exp(fresh - highest)
    weight_total = jnp.sum(weights, axis=3) + fresh_weight
    rounded = lax.optimization_barrier(weights.astype(jnp.bfloat16)).astype(jnp.float32)
    rounded_fresh = lax.optimization_barrier(fresh_weight.astype(jnp.bfloat16)).astype(jnp.float32)
    mixed = jnp.einsum("rkgc,rckd->rkgd", rounded, values_old)
    mixed = mixed + rounded_fresh[..., None] * values_now[:, :, None, :]
    attended = (mixed / weight_total[..., None]).astype(jnp.bfloat16)
    return attended.reshape(row_count, QUERY_HEADS * HEAD_WIDTH)


def reference(queries, incoming_keys, incoming_values, cached_key_rows, cached_value_rows, cache_length, adapter_of_row, adapter_slot_table, output_projection, adapter_down_weights, adapter_up_weights):
    attended = attention_rows(queries, incoming_keys, incoming_values, cached_key_rows, cached_value_rows, cache_length)
    base = jnp.dot(attended, output_projection, preferred_element_type=jnp.float32)
    slot_of_row = adapter_slot_table[adapter_of_row].astype(jnp.int32)

    def shrink_row(paired):
        row_in, storage_slot_input = paired
        down_matrix = lax.dynamic_index_in_dim(adapter_down_weights, storage_slot_input, 0, False)
        return jnp.dot(row_in, down_matrix, preferred_element_type=jnp.float32)

    shrunk = lax.map(shrink_row, (attended, slot_of_row)).astype(jnp.bfloat16)

    def expand_row(paired):
        row_in, storage_slot_input = paired
        up_matrix = lax.dynamic_index_in_dim(adapter_up_weights, storage_slot_input, 0, False)
        return jnp.dot(row_in, up_matrix, preferred_element_type=jnp.float32)

    delta = lax.map(expand_row, (shrunk, slot_of_row)).astype(jnp.bfloat16)
    return (base + delta.astype(jnp.float32)).astype(jnp.bfloat16)
```

```python
import jax
import jax.numpy as jnp
from jax import lax
from jax.experimental import pallas as pl
from jax.experimental.pallas import tpu as pltpu
from jax.sharding import PartitionSpec as P

QUERY_HEADS = 32
KV_HEADS = 4
HEAD_WIDTH = 128
CAP = 64
LANES = 128


def attend_kernel(
    column_ref, length_ref, query_ref, key_now_ref, value_now_ref, key_ref, value_ref, out_ref
):
    block = query_ref.shape[0]
    heads = query_ref.shape[1] // HEAD_WIDTH
    context = key_ref.shape[1]
    rows = LANES // heads
    copies = LANES // context
    first_row = pl.program_id(0) * block
    lane = lax.broadcasted_iota(jnp.int32, (1, LANES), 1)
    lane_row = lax.rem(lane, rows)
    row_masks = [lane_row == r for r in range(rows)]
    place = lax.broadcasted_iota(jnp.int32, (context, LANES), 0)
    side = lax.broadcasted_iota(jnp.int32, (LANES, LANES), 0)
    across = lax.broadcasted_iota(jnp.int32, (LANES, LANES), 1)
    fresh_mask = side == lax.rem(across, rows)
    offset = lax.rem(side, rows) - across // context
    score_scale = HEAD_WIDTH ** (-0.5)
    contract_last = (((1,), (1,)), ((), ()))
    for group in range(block // rows):
        at = slice(group * rows, (group + 1) * rows)
        stacked = jnp.concatenate(
            [query_ref[at, h * HEAD_WIDTH : (h + 1) * HEAD_WIDTH] for h in range(heads)], axis=0
        )
        keys = key_ref[at].reshape(rows * context, HEAD_WIDTH)
        wide = lax.dot_general(
            keys, stacked, contract_last, preferred_element_type=jnp.float32
        ).reshape(rows, context, LANES)
        lengths = jnp.zeros((1, LANES), jnp.int32)
        scores = wide[0]
        for r in range(rows):
            lengths = jnp.where(row_masks[r], length_ref[first_row + group * rows + r], lengths)
            scores = jnp.where(row_masks[r], wide[r], scores)
        now = lax.dot_general(
            key_now_ref[at], stacked, contract_last, preferred_element_type=jnp.float32
        )
        fresh = jnp.sum(jnp.where(fresh_mask[:rows], now, 0.0), axis=0, keepdims=True)
        fresh = fresh * score_scale
        scores = jnp.where(place < lengths, scores * score_scale, -1e30)
        highest = jnp.maximum(jnp.max(scores, axis=0, keepdims=True), fresh)
        weights = jnp.exp(scores - highest)
        fresh_weight = jnp.exp(fresh - highest)
        total = jnp.sum(weights, axis=0, keepdims=True) + fresh_weight
        turned = jnp.transpose(jnp.concatenate([weights] * copies, axis=0))
        extra = jnp.where(side < rows, jnp.where(fresh_mask, fresh_weight, 0.0), total)
        extra = jnp.transpose(extra)
        spread = jnp.concatenate(
            [
                jnp.where(offset == t * copies, turned, 0.0).astype(jnp.bfloat16)
                for t in range(rows // copies)
            ],
            axis=1,
        )
        values = value_ref[at].reshape(rows * context, HEAD_WIDTH)
        mixed = jnp.dot(spread, values, preferred_element_type=jnp.float32)
        mixed = mixed + jnp.dot(
            extra[:, :rows].astype(jnp.bfloat16),
            value_now_ref[at],
            preferred_element_type=jnp.float32,
        )
        attended = (mixed / extra[:, rows : rows + 1]).astype(jnp.bfloat16)
        for h in range(heads):
            out_ref[at, h * HEAD_WIDTH : (h + 1) * HEAD_WIDTH] = attended[h * rows : (h + 1) * rows]


def attend_local(
    queries, incoming_keys, incoming_values, cached_key_rows, cached_value_rows, cache_length
):
    row_count, feat_count = queries.shape
    context = cached_key_rows.shape[1]
    heads = feat_count // HEAD_WIDTH
    first_kv = lax.axis_index("sub") * heads // (QUERY_HEADS // KV_HEADS)
    column = first_kv.astype(jnp.int32).reshape(1)
    block = 64
    now_spec = pl.BlockSpec((block, HEAD_WIDTH), lambda i, c, n: (i, c[0]))
    old_spec = pl.BlockSpec((block, context, HEAD_WIDTH), lambda i, c, n: (i, 0, c[0]))
    row_spec = pl.BlockSpec((block, feat_count), lambda i, c, n: (i, 0))
    return pl.pallas_call(
        attend_kernel,
        grid_spec=pltpu.PrefetchScalarGridSpec(
            num_scalar_prefetch=2,
            grid=(row_count // block,),
            in_specs=[row_spec, now_spec, now_spec, old_spec, old_spec],
            out_specs=row_spec,
        ),
        out_shape=jax.ShapeDtypeStruct((row_count, feat_count), jnp.bfloat16),
        name="attend",
    )(
        column,
        cache_length,
        queries,
        incoming_keys,
        incoming_values,
        cached_key_rows,
        cached_value_rows,
    )


def grouped_product(rows_by_adapter, weights, group_sizes, leading_extent):
    total_rows = rows_by_adapter.shape[0]
    shifted = jnp.roll(rows_by_adapter, -leading_extent, axis=0)
    result = lax.ragged_dot(shifted, weights, group_sizes, preferred_element_type=jnp.float32)
    used = lax.broadcasted_iota(jnp.int32, (total_rows, 1), 0) < jnp.sum(group_sizes)
    result = jnp.where(used, result, 0.0)
    return jnp.roll(result, leading_extent, axis=0)


def on_device(
    queries,
    incoming_keys,
    incoming_values,
    cached_key_rows,
    cached_value_rows,
    cache_length,
    adapter_of_row,
    adapter_slot_table,
    output_projection,
    adapter_down_weights,
    adapter_up_weights,
):
    row_count = queries.shape[0]
    feat_count = queries.shape[1]
    attended = attend_local(
        queries, incoming_keys, incoming_values, cached_key_rows, cached_value_rows, cache_length
    )
    partial_out = jnp.dot(attended, output_projection, preferred_element_type=jnp.float32)
    base = lax.psum_scatter(partial_out, ("tensor", "sub"), scatter_dimension=1, tiled=True)
    output_columns = adapter_up_weights.shape[2]
    adp_local = adapter_down_weights.shape[0]
    adapter_count = adapter_slot_table.shape[0]
    matched = adapter_of_row[:, None] == lax.broadcasted_iota(
        jnp.int32, (row_count, adapter_count), 1
    )
    slot_of_row = jnp.sum(jnp.where(matched, adapter_slot_table[None, :], 0), axis=1)
    owners = lax.axis_size("replica")
    owner_of_row = slot_of_row // adp_local
    local_id = slot_of_row - owner_of_row * adp_local
    by_owner = (
        owner_of_row[:, None] == lax.broadcasted_iota(jnp.int32, (row_count, owners), 1)
    ).astype(jnp.int32)
    earlier = jnp.cumsum(by_owner, axis=0) - by_owner
    position = jnp.sum(earlier * by_owner, axis=1)
    target = owner_of_row * CAP + position
    slot_total = owners * CAP
    route_map = (
        target[:, None] == lax.broadcasted_iota(jnp.int32, (row_count, slot_total), 1)
    ).astype(jnp.bfloat16)
    outgoing = jnp.einsum("rs,rf->sf", route_map, attended, preferred_element_type=jnp.float32)
    outgoing = outgoing.astype(jnp.bfloat16).reshape(owners, CAP, feat_count)
    labels = jnp.einsum(
        "rs,r->s",
        route_map,
        (local_id + 1).astype(jnp.bfloat16),
        preferred_element_type=jnp.float32,
    )
    labels = labels.astype(jnp.bfloat16).reshape(owners, CAP)
    arrived, arrived_labels = (
        lax.all_to_all(outgoing, "replica", split_axis=0, concat_axis=0, tiled=True),
        lax.all_to_all(labels, "replica", split_axis=0, concat_axis=0, tiled=True),
    )
    arrived_rows = arrived.reshape(slot_total, feat_count)
    label_ids = arrived_labels.reshape(slot_total).astype(jnp.int32)
    sort_keys = jnp.where(label_ids == 0, adp_local + 1, label_ids)
    order_in = jnp.argsort(sort_keys, stable=True)
    inverse_in = jnp.argsort(order_in, stable=True)
    sorted_in = arrived_rows[order_in]
    wanted = lax.broadcasted_iota(jnp.int32, (1, adp_local), 1) + 1
    sizes_in = jnp.sum((label_ids[:, None] == wanted).astype(jnp.int32), axis=0)
    rank_part = grouped_product(sorted_in, adapter_down_weights, sizes_in, 0)
    shrunk_in = lax.psum(rank_part, ("tensor", "sub")).astype(jnp.bfloat16)
    delta_sorted = grouped_product(shrunk_in, adapter_up_weights, sizes_in, 0).astype(jnp.bfloat16)
    delta_in = delta_sorted[inverse_in].reshape(owners, CAP, output_columns)
    returned = lax.all_to_all(delta_in, "replica", split_axis=0, concat_axis=0, tiled=True)
    delta = jnp.einsum(
        "rs,sc->rc",
        route_map,
        returned.reshape(slot_total, output_columns),
        preferred_element_type=jnp.float32,
    )
    delta = delta.astype(jnp.bfloat16)
    return (base + delta.astype(jnp.float32)).astype(jnp.bfloat16)


def solution(mesh):
    return jax.shard_map(
        on_device,
        mesh=mesh,
        in_specs=(
            P(("group", "replica"), ("tensor", "sub")),
            P(("group", "replica"), "tensor"),
            P(("group", "replica"), "tensor"),
            P(("group", "replica"), None, "tensor"),
            P(("group", "replica"), None, "tensor"),
            P(("group", "replica")),
            P(("group", "replica")),
            P("group"),
            P(("tensor", "sub"), None),
            P("replica", ("tensor", "sub"), None),
            P("replica", None, ("tensor", "sub")),
        ),
        out_specs=P(("group", "replica"), ("tensor", "sub")),
        check_vma=False,
    )
```

```python
import functools

import jax
import jax.numpy as jnp
from jax import lax
from jax.experimental import pallas as pl
from jax.experimental.pallas import tpu as pltpu
from jax.sharding import PartitionSpec as P

QUERY_HEADS = 32
KV_HEADS = 4
HEAD_WIDTH = 128
CAP = 64
LANES = 128
MESH = pl.DeviceIdType.MESH


def attend_kernel(
    column_ref, length_ref, query_ref, key_now_ref, value_now_ref, key_ref, value_ref, out_ref
):
    block = query_ref.shape[0]
    heads = query_ref.shape[1] // HEAD_WIDTH
    context = key_ref.shape[1]
    rows = LANES // heads
    copies = LANES // context
    first_row = pl.program_id(0) * block
    lane = lax.broadcasted_iota(jnp.int32, (1, LANES), 1)
    lane_row = lax.rem(lane, rows)
    row_masks = [lane_row == r for r in range(rows)]
    place = lax.broadcasted_iota(jnp.int32, (context, LANES), 0)
    side = lax.broadcasted_iota(jnp.int32, (LANES, LANES), 0)
    across = lax.broadcasted_iota(jnp.int32, (LANES, LANES), 1)
    fresh_mask = side == lax.rem(across, rows)
    offset = lax.rem(side, rows) - across // context
    score_scale = HEAD_WIDTH ** (-0.5)
    contract_last = (((1,), (1,)), ((), ()))
    for group in range(block // rows):
        at = slice(group * rows, (group + 1) * rows)
        stacked = jnp.concatenate(
            [query_ref[at, h * HEAD_WIDTH : (h + 1) * HEAD_WIDTH] for h in range(heads)], axis=0
        )
        keys = key_ref[at].reshape(rows * context, HEAD_WIDTH)
        wide = lax.dot_general(
            keys, stacked, contract_last, preferred_element_type=jnp.float32
        ).reshape(rows, context, LANES)
        lengths = jnp.zeros((1, LANES), jnp.int32)
        scores = wide[0]
        for r in range(rows):
            lengths = jnp.where(row_masks[r], length_ref[first_row + group * rows + r], lengths)
            scores = jnp.where(row_masks[r], wide[r], scores)
        now = lax.dot_general(
            key_now_ref[at], stacked, contract_last, preferred_element_type=jnp.float32
        )
        fresh = jnp.sum(jnp.where(fresh_mask[:rows], now, 0.0), axis=0, keepdims=True)
        fresh = fresh * score_scale
        scores = jnp.where(place < lengths, scores * score_scale, -1e30)
        highest = jnp.maximum(jnp.max(scores, axis=0, keepdims=True), fresh)
        weights = jnp.exp(scores - highest)
        fresh_weight = jnp.exp(fresh - highest)
        total = jnp.sum(weights, axis=0, keepdims=True) + fresh_weight
        turned = jnp.transpose(jnp.concatenate([weights] * copies, axis=0))
        extra = jnp.where(side < rows, jnp.where(fresh_mask, fresh_weight, 0.0), total)
        extra = jnp.transpose(extra)
        spread = jnp.concatenate(
            [
                jnp.where(offset == t * copies, turned, 0.0).astype(jnp.bfloat16)
                for t in range(rows // copies)
            ],
            axis=1,
        )
        values = value_ref[at].reshape(rows * context, HEAD_WIDTH)
        mixed = jnp.dot(spread, values, preferred_element_type=jnp.float32)
        mixed = mixed + jnp.dot(
            extra[:, :rows].astype(jnp.bfloat16),
            value_now_ref[at],
            preferred_element_type=jnp.float32,
        )
        attended = (mixed / extra[:, rows : rows + 1]).astype(jnp.bfloat16)
        for h in range(heads):
            out_ref[at, h * HEAD_WIDTH : (h + 1) * HEAD_WIDTH] = attended[h * rows : (h + 1) * rows]


def attend_local(
    queries, incoming_keys, incoming_values, cached_key_rows, cached_value_rows, cache_length
):
    row_count, feat_count = queries.shape
    context = cached_key_rows.shape[1]
    heads = feat_count // HEAD_WIDTH
    first_kv = lax.axis_index("sub") * heads // (QUERY_HEADS // KV_HEADS)
    column = first_kv.astype(jnp.int32).reshape(1)
    block = 64
    now_spec = pl.BlockSpec((block, HEAD_WIDTH), lambda i, c, n: (i, c[0]))
    old_spec = pl.BlockSpec((block, context, HEAD_WIDTH), lambda i, c, n: (i, 0, c[0]))
    row_spec = pl.BlockSpec((block, feat_count), lambda i, c, n: (i, 0))
    return pl.pallas_call(
        attend_kernel,
        grid_spec=pltpu.PrefetchScalarGridSpec(
            num_scalar_prefetch=2,
            grid=(row_count // block,),
            in_specs=[row_spec, now_spec, now_spec, old_spec, old_spec],
            out_specs=row_spec,
        ),
        out_shape=jax.ShapeDtypeStruct((row_count, feat_count), jnp.bfloat16),
        name="attend",
    )(
        column,
        cache_length,
        queries,
        incoming_keys,
        incoming_values,
        cached_key_rows,
        cached_value_rows,
    )


def project_kernel(
    tensors,
    owners,
    table_ref,
    adapter_ref,
    attended_ref,
    projection_ref,
    down_ref,
    up_ref,
    out_ref,
    panel,
    pair_out,
    pair_in,
    cross_out,
    cross_in,
    base,
    route_out,
    route_in,
    rank_out,
    rank_in,
    delta_out,
    delta_in,
    gather,
    panel_sem,
    pair_send,
    pair_recv,
    cross_send,
    cross_recv,
    route_send,
    route_recv,
    rank_send,
    rank_recv,
    delta_send,
    delta_recv,
):
    bf16, f32 = jnp.bfloat16, jnp.float32
    replica = lax.axis_index("replica")
    tensor = lax.axis_index("tensor")
    sub = lax.axis_index("sub")
    rows, feats = attended_ref.shape
    chunk = panel.shape[2]
    columns = out_ref.shape[1]
    chunks = columns // chunk
    peers = tensors * 2
    far = (tensors - 1) * chunks
    adp_local, _, rank = down_ref.shape
    place = tensor * 2 + sub

    def tensor_peer(e):
        other = lax.rem(place + e, peers)
        return {"tensor": other // 2, "sub": lax.rem(other, 2)}

    barrier = pltpu.get_barrier_semaphore()
    for e in range(1, peers):
        pl.semaphore_signal(barrier, inc=1, device_id=tensor_peer(e), device_id_type=MESH)
    for d in range(1, owners):
        pl.semaphore_signal(
            barrier, inc=1, device_id={"replica": lax.rem(replica + d, owners)}, device_id_type=MESH
        )

    def panel_copy(slot, other_tensor, other_sub, c):
        start = pl.multiple_of((other_tensor * 2 + other_sub) * columns + c * chunk, chunk)
        return pltpu.make_async_copy(
            projection_ref.at[:, pl.ds(start, chunk)], panel.at[slot], panel_sem.at[slot]
        )

    def far_panel(i, mine):
        other = lax.rem(tensor + 1 + i // chunks, tensors)
        side = sub if mine else 1 - sub
        return panel_copy(i + (far if mine else 0), other, side, lax.rem(i, chunks))

    def near_panel(c, mine):
        side = sub if mine else 1 - sub
        return panel_copy(2 * far + (chunks if mine else 0) + c, tensor, side, c)

    for i in range(far):
        far_panel(i, False).start()
    for i in range(far):
        far_panel(i, True).start()
    for c in range(chunks):
        near_panel(c, False).start()
    for c in range(chunks):
        near_panel(c, True).start()

    slots = owners * CAP
    adapters = adapter_ref[...]
    stored = jnp.zeros_like(adapters)
    for a in range(table_ref.shape[0]):
        stored = jnp.where(adapters == a, table_ref[a], stored)
    owner = stored // adp_local
    local = stored - owner * adp_local
    step = lax.rem(owner - replica + owners, owners)
    by_owner = lax.broadcasted_iota(jnp.int32, (max(owners, 8), rows), 0) == step
    before = lax.broadcasted_iota(jnp.int32, (rows, rows), 0) < lax.broadcasted_iota(
        jnp.int32, (rows, rows), 1
    )
    by_owner = jnp.where(by_owner, 1.0, 0.0)
    earlier = jnp.dot(
        by_owner.astype(bf16), jnp.where(before, 1.0, 0.0).astype(bf16), preferred_element_type=f32
    )
    position = jnp.sum(by_owner * earlier, axis=0, keepdims=True)
    target = step.astype(f32) * CAP + position
    slot_at = lax.broadcasted_iota(jnp.int32, (slots, rows), 0).astype(f32)
    route = jnp.where(slot_at == target, 1.0, 0.0)
    gather[...] = jnp.transpose(route).astype(bf16)
    route = route.astype(bf16)
    label = lax.broadcasted_iota(jnp.int32, (LANES, rows), 0) == local
    label = jnp.where(label, 1.0, 0.0).astype(bf16)
    labels = lax.dot_general(
        route, label, (((1,), (1,)), ((), ())), preferred_element_type=f32
    ).astype(bf16)
    routed = jnp.dot(route, attended_ref[...], preferred_element_type=f32).astype(bf16)
    for d in range(owners):
        into = route_out.at[d] if d else route_in.at[0]
        into[:, :feats] = routed[d * CAP : (d + 1) * CAP]
        into[:, feats:] = labels[d * CAP : (d + 1) * CAP]

    pl.semaphore_wait(barrier, peers - 1 + owners - 1)

    def route_copy(d):
        return pltpu.make_async_remote_copy(
            src_ref=route_out.at[d],
            dst_ref=route_in.at[d],
            send_sem=route_send.at[d],
            recv_sem=route_recv.at[d],
            device_id={"replica": lax.rem(replica + d, owners)},
            device_id_type=MESH,
        )

    def delta_copy(d):
        return pltpu.make_async_remote_copy(
            src_ref=delta_out.at[d],
            dst_ref=delta_in.at[d],
            send_sem=delta_send.at[d],
            recv_sem=delta_recv.at[d],
            device_id={"replica": lax.rem(replica - d + owners, owners)},
            device_id_type=MESH,
        )

    def rank_copy(e):
        return pltpu.make_async_remote_copy(
            src_ref=rank_out,
            dst_ref=rank_in.at[e],
            send_sem=rank_send.at[e],
            recv_sem=rank_recv.at[e],
            device_id=tensor_peer(e),
            device_id_type=MESH,
        )

    def pair_copy(i):
        return pltpu.make_async_remote_copy(
            src_ref=pair_out.at[i],
            dst_ref=pair_in.at[i],
            send_sem=pair_send.at[i],
            recv_sem=pair_recv.at[i],
            device_id={"sub": 1 - sub},
            device_id_type=MESH,
        )

    def cross_copy(i):
        return pltpu.make_async_remote_copy(
            src_ref=cross_out.at[i],
            dst_ref=cross_in.at[i],
            send_sem=cross_send.at[i],
            recv_sem=cross_recv.at[i],
            device_id={"tensor": lax.rem(tensor + 1 + i // chunks, tensors)},
            device_id_type=MESH,
        )

    for d in reversed(range(1, owners)):
        route_copy(d).start()

    def product(slot):
        return jnp.dot(attended_ref[...], panel[slot], preferred_element_type=f32)

    def far_pair(i, carry):
        far_panel(i, False).wait()
        pair_out[i] = product(i).astype(bf16)
        pair_copy(i).start()
        return carry

    def far_mine(i, carry):
        far_panel(i, True).wait()
        mine = product(far + i)
        pair_copy(i).wait_recv()
        cross_out[i] = (mine + pair_in[i].astype(f32)).astype(bf16)
        return carry

    def far_send(i, carry):
        cross_copy(i).start()
        return carry

    def far_both(i, carry):
        return far_send(i, far_mine(i, carry))

    def near_pair(c, carry):
        near_panel(c, False).wait()
        pair_out[far + c] = product(2 * far + c).astype(bf16)
        pair_copy(far + c).start()
        return carry

    def near_mine(c, carry):
        near_panel(c, True).wait()
        base[c] = product(2 * far + chunks + c)
        return carry

    half = far // 2
    lax.fori_loop(0, far, far_pair, 0)
    lax.fori_loop(0, half, far_both, 0)
    lax.fori_loop(half, far, far_mine, 0)
    lax.fori_loop(0, chunks, near_pair, 0)
    lax.fori_loop(0, chunks, near_mine, 0)

    for d in reversed(range(1, owners)):
        route_copy(d).wait_recv()
    arrived = route_in[:, :, :feats].reshape(slots, feats)
    marks = route_in[:, :, feats:].reshape(slots, LANES)
    shrunk = jnp.zeros((slots, rank), f32)
    for a in range(adp_local):
        part = jnp.dot(arrived, down_ref[a], preferred_element_type=f32)
        shrunk = shrunk + jnp.where(marks[:, a : a + 1].astype(f32) > 0.5, part, 0.0)
    rank_out[...] = shrunk.astype(bf16)
    for e in range(1, peers):
        rank_copy(e).start()
    wide = adp_local * rank
    spread = lax.broadcasted_iota(jnp.int32, (LANES, wide), 0) == (
        lax.broadcasted_iota(jnp.int32, (LANES, wide), 1) // rank
    )
    mask = jnp.dot(marks, jnp.where(spread, 1.0, 0.0).astype(bf16), preferred_element_type=f32)
    repeat = lax.broadcasted_iota(jnp.int32, (rank, wide), 0) == lax.rem(
        lax.broadcasted_iota(jnp.int32, (rank, wide), 1), rank
    )
    repeat = jnp.where(repeat, 1.0, 0.0).astype(bf16)
    for e in range(1, peers):
        rank_copy(e).wait_recv()
        shrunk = shrunk + rank_in[e].astype(f32)
    lax.fori_loop(half, far, far_send, 0)
    held = jnp.dot(shrunk.astype(bf16), repeat, preferred_element_type=f32)
    held = jnp.where(mask > 0.5, held, 0.0).astype(bf16)
    for d in reversed(range(owners)):
        into = delta_out if d else delta_in
        into[d] = jnp.dot(
            held[d * CAP : (d + 1) * CAP], up_ref[...], preferred_element_type=f32
        ).astype(bf16)
        if d:
            delta_copy(d).start()

    def near_add(c, carry):
        pair_copy(far + c).wait_recv()
        base[c] = base[c] + pair_in[far + c].astype(f32)
        return carry

    def far_add(i, carry):
        cross_copy(i).wait_recv()
        c = lax.rem(i, chunks)
        base[c] = base[c] + cross_in[i].astype(f32)
        return carry

    lax.fori_loop(0, chunks, near_add, 0)
    lax.fori_loop(0, far, far_add, 0)
    for d in range(1, owners):
        delta_copy(d).wait_recv()
    for c in range(chunks):
        at = slice(c * chunk, (c + 1) * chunk)
        delta = jnp.dot(
            gather[...], delta_in[:, :, at].reshape(slots, chunk), preferred_element_type=f32
        )
        out_ref[:, at] = (base[c] + delta).astype(bf16)

    for d in range(1, owners):
        route_copy(d).wait_send()
        delta_copy(d).wait_send()
    for e in range(1, peers):
        rank_copy(e).wait_send()

    def pair_sent(i, carry):
        pair_copy(i).wait_send()
        return carry

    def cross_sent(i, carry):
        cross_copy(i).wait_send()
        return carry

    lax.fori_loop(0, far + chunks, pair_sent, 0)
    lax.fori_loop(0, far, cross_sent, 0)


def on_device(
    queries,
    incoming_keys,
    incoming_values,
    cached_key_rows,
    cached_value_rows,
    cache_length,
    adapter_of_row,
    adapter_slot_table,
    output_projection,
    adapter_down_weights,
    adapter_up_weights,
):
    attended = attend_local(
        queries, incoming_keys, incoming_values, cached_key_rows, cached_value_rows, cache_length
    )
    rows, feats = attended.shape
    adp_local, _, rank = adapter_down_weights.shape
    columns = adapter_up_weights.shape[2]
    tensors = lax.axis_size("tensor")
    owners = lax.axis_size("replica")
    peers = tensors * lax.axis_size("sub")
    chunk = min(512, columns)
    chunks = columns // chunk
    far = (tensors - 1) * chunks
    bf16 = jnp.bfloat16
    vmem = pl.BlockSpec(memory_space=pltpu.VMEM)
    dma = pltpu.SemaphoreType.DMA
    return pl.pallas_call(
        functools.partial(project_kernel, tensors, owners),
        out_shape=jax.ShapeDtypeStruct((rows, columns), bf16),
        in_specs=[
            pl.BlockSpec(memory_space=pltpu.SMEM),
            vmem,
            vmem,
            pl.BlockSpec(memory_space=pl.ANY),
            vmem,
            vmem,
        ],
        out_specs=vmem,
        scratch_shapes=[
            pltpu.VMEM((peers * chunks, feats, chunk), bf16),
            pltpu.VMEM((far + chunks, rows, chunk), bf16),
            pltpu.VMEM((far + chunks, rows, chunk), bf16),
            pltpu.VMEM((far, rows, chunk), bf16),
            pltpu.VMEM((far, rows, chunk), bf16),
            pltpu.VMEM((chunks, rows, chunk), jnp.float32),
            pltpu.VMEM((owners, CAP, feats + LANES), bf16),
            pltpu.VMEM((owners, CAP, feats + LANES), bf16),
            pltpu.VMEM((owners * CAP, rank), bf16),
            pltpu.VMEM((peers, owners * CAP, rank), bf16),
            pltpu.VMEM((owners, CAP, columns), bf16),
            pltpu.VMEM((owners, CAP, columns), bf16),
            pltpu.VMEM((rows, owners * CAP), bf16),
            dma((peers * chunks,)),
            dma((far + chunks,)),
            dma((far + chunks,)),
            dma((far,)),
            dma((far,)),
            dma((owners,)),
            dma((owners,)),
            dma((peers,)),
            dma((peers,)),
            dma((owners,)),
            dma((owners,)),
        ],
        compiler_params=pltpu.CompilerParams(
            collective_id=0, has_side_effects=True, vmem_limit_bytes=52 * 1024 * 1024
        ),
        name="project",
    )(
        adapter_slot_table,
        adapter_of_row.reshape(1, rows),
        attended,
        output_projection,
        adapter_down_weights,
        adapter_up_weights.reshape(adp_local * rank, columns),
    )


def solution(mesh):
    return jax.shard_map(
        on_device,
        mesh=mesh,
        in_specs=(
            P(("group", "replica"), ("tensor", "sub")),
            P(("group", "replica"), "tensor"),
            P(("group", "replica"), "tensor"),
            P(("group", "replica"), None, "tensor"),
            P(("group", "replica"), None, "tensor"),
            P(("group", "replica")),
            P(("group", "replica")),
            P("group"),
            P(("tensor", "sub"), None),
            P("replica", ("tensor", "sub"), None),
            P("replica", None, ("tensor", "sub")),
        ),
        out_specs=P(("group", "replica"), ("tensor", "sub")),
        check_vma=False,
    )
```

```python
import functools

import jax
import jax.numpy as jnp
from jax import lax
from jax.experimental import pallas as pl
from jax.experimental.pallas import tpu as pltpu
from jax.sharding import PartitionSpec as P

QUERY_HEADS = 32
KV_HEADS = 4
HEAD_WIDTH = 128
CAP = 64
LANES = 128
PARTS = 2
MESH = pl.DeviceIdType.MESH


def attend_block(
    first_row, block, length_ref, query_ref, key_now_ref, value_now_ref, key_ref, value_ref, out_ref
):
    heads = query_ref.shape[1] // HEAD_WIDTH
    context = key_ref.shape[1]
    rows = LANES // heads
    copies = LANES // context
    lane = lax.broadcasted_iota(jnp.int32, (1, LANES), 1)
    lane_row = lax.rem(lane, rows)
    row_masks = [lane_row == r for r in range(rows)]
    place = lax.broadcasted_iota(jnp.int32, (context, LANES), 0)
    side = lax.broadcasted_iota(jnp.int32, (LANES, LANES), 0)
    across = lax.broadcasted_iota(jnp.int32, (LANES, LANES), 1)
    fresh_mask = side == lax.rem(across, rows)
    offset = lax.rem(side, rows) - across // context
    score_scale = HEAD_WIDTH ** (-0.5)
    contract_last = (((1,), (1,)), ((), ()))
    for group in range(block // rows):
        at = pl.ds(pl.multiple_of(first_row + group * rows, rows), rows)
        stacked = jnp.concatenate(
            [query_ref[at, h * HEAD_WIDTH : (h + 1) * HEAD_WIDTH] for h in range(heads)], axis=0
        )
        keys = key_ref[at].reshape(rows * context, HEAD_WIDTH)
        wide = lax.dot_general(
            keys, stacked, contract_last, preferred_element_type=jnp.float32
        ).reshape(rows, context, LANES)
        lengths = jnp.zeros((1, LANES), jnp.int32)
        scores = wide[0]
        for r in range(rows):
            lengths = jnp.where(row_masks[r], length_ref[first_row + group * rows + r], lengths)
            scores = jnp.where(row_masks[r], wide[r], scores)
        now = lax.dot_general(
            key_now_ref[at], stacked, contract_last, preferred_element_type=jnp.float32
        )
        fresh = jnp.sum(jnp.where(fresh_mask[:rows], now, 0.0), axis=0, keepdims=True)
        fresh = fresh * score_scale
        scores = jnp.where(place < lengths, scores * score_scale, -1e30)
        highest = jnp.maximum(jnp.max(scores, axis=0, keepdims=True), fresh)
        weights = jnp.exp(scores - highest)
        fresh_weight = jnp.exp(fresh - highest)
        total = jnp.sum(weights, axis=0, keepdims=True) + fresh_weight
        turned = jnp.transpose(jnp.concatenate([weights] * copies, axis=0))
        extra = jnp.where(side < rows, jnp.where(fresh_mask, fresh_weight, 0.0), total)
        extra = jnp.transpose(extra)
        spread = jnp.concatenate(
            [
                jnp.where(offset == t * copies, turned, 0.0).astype(jnp.bfloat16)
                for t in range(rows // copies)
            ],
            axis=1,
        )
        values = value_ref[at].reshape(rows * context, HEAD_WIDTH)
        mixed = jnp.dot(spread, values, preferred_element_type=jnp.float32)
        mixed = mixed + jnp.dot(
            extra[:, :rows].astype(jnp.bfloat16),
            value_now_ref[at],
            preferred_element_type=jnp.float32,
        )
        attended = (mixed / extra[:, rows : rows + 1]).astype(jnp.bfloat16)
        for h in range(heads):
            out_ref[at, h * HEAD_WIDTH : (h + 1) * HEAD_WIDTH] = attended[h * rows : (h + 1) * rows]


def project_kernel(
    tensors,
    owners,
    table_ref,
    length_ref,
    adapter_ref,
    query_ref,
    fresh_key_ref,
    fresh_value_ref,
    stored_key_ref,
    stored_value_ref,
    projection_ref,
    stored_down_ref,
    stored_up_ref,
    out_ref,
    key_now_ref,
    value_now_ref,
    key_ref,
    value_ref,
    down_ref,
    up_ref,
    attended_ref,
    panel,
    pair_out,
    pair_in,
    cross_out,
    cross_in,
    base,
    route_out,
    route_in,
    label_out,
    label_in,
    rank_out,
    rank_in,
    delta_out,
    delta_in,
    gather,
    cache_sem,
    weight_sem,
    panel_sem,
    pair_send,
    pair_recv,
    cross_send,
    cross_recv,
    route_send,
    route_recv,
    label_send,
    label_recv,
    rank_send,
    rank_recv,
    delta_send,
    delta_recv,
):
    bf16, f32 = jnp.bfloat16, jnp.float32
    replica = lax.axis_index("replica")
    tensor = lax.axis_index("tensor")
    sub = lax.axis_index("sub")
    rows, feats = attended_ref.shape
    block = min(64, rows)
    heads = feats // HEAD_WIDTH
    head_at = pl.ds(
        pl.multiple_of(sub * heads // (QUERY_HEADS // KV_HEADS) * HEAD_WIDTH, HEAD_WIDTH), HEAD_WIDTH
    )
    chunk = panel.shape[2]
    columns = out_ref.shape[1]
    chunks = columns // chunk
    peers = tensors * 2
    far = (tensors - 1) * chunks
    rank = rank_out.shape[2]
    wide = down_ref.shape[0]
    adp_local = wide // rank
    part_cap = CAP // PARTS
    part_slots = owners * part_cap
    place = tensor * 2 + sub

    def tensor_peer(e):
        other = lax.rem(place + e, peers)
        return {"tensor": other // 2, "sub": lax.rem(other, 2)}

    barrier = pltpu.get_barrier_semaphore()
    for e in range(1, peers):
        pl.semaphore_signal(barrier, inc=1, device_id=tensor_peer(e), device_id_type=MESH)
    for d in range(1, owners):
        pl.semaphore_signal(
            barrier, inc=1, device_id={"replica": lax.rem(replica + d, owners)}, device_id_type=MESH
        )

    def panel_copy(slot, other_tensor, other_sub, c):
        start = pl.multiple_of((other_tensor * 2 + other_sub) * columns + c * chunk, chunk)
        return pltpu.make_async_copy(
            projection_ref.at[:, pl.ds(start, chunk)], panel.at[slot], panel_sem.at[slot]
        )

    def far_panel(i, mine):
        other = lax.rem(tensor + 1 + i // chunks, tensors)
        side = sub if mine else 1 - sub
        return panel_copy(i + (far if mine else 0), other, side, lax.rem(i, chunks))

    def near_panel(c, mine):
        side = sub if mine else 1 - sub
        return panel_copy(2 * far + (chunks if mine else 0) + c, tensor, side, c)

    def cache_copies(i):
        at = pl.ds(pl.multiple_of(i * block, block), block)
        return [
            pltpu.make_async_copy(
                stored.at[at, :, head_at], kept.at[at], cache_sem.at[2 * i + which]
            )
            for which, (stored, kept) in enumerate(
                [(stored_key_ref, key_ref), (stored_value_ref, value_ref)]
            )
        ]

    weight_copies = [
        pltpu.make_async_copy(stored_down_ref, down_ref, weight_sem.at[0]),
        pltpu.make_async_copy(stored_up_ref, up_ref, weight_sem.at[1]),
    ]
    now_copies = [
        pltpu.make_async_copy(fresh_key_ref.at[:, head_at], key_now_ref, weight_sem.at[2]),
        pltpu.make_async_copy(fresh_value_ref.at[:, head_at], value_now_ref, weight_sem.at[3]),
    ]
    for copy in now_copies:
        copy.start()
    for i in range(rows // block):
        for copy in cache_copies(i):
            copy.start()
    for i in range(far):
        far_panel(i, False).start()
    for i in range(far):
        far_panel(i, True).start()
    for c in range(chunks):
        near_panel(c, False).start()
    for c in range(chunks):
        near_panel(c, True).start()
    for copy in weight_copies:
        copy.start()

    slots = owners * CAP
    adapters = adapter_ref[...]
    stored = jnp.zeros_like(adapters)
    for a in range(table_ref.shape[0]):
        stored = jnp.where(adapters == a, table_ref[a], stored)
    owner = stored // adp_local
    local = stored - owner * adp_local
    step = lax.rem(owner - replica + owners, owners)
    by_owner = lax.broadcasted_iota(jnp.int32, (max(owners, 8), rows), 0) == step
    before = lax.broadcasted_iota(jnp.int32, (rows, rows), 0) < lax.broadcasted_iota(
        jnp.int32, (rows, rows), 1
    )
    by_owner = jnp.where(by_owner, 1.0, 0.0)
    earlier = jnp.dot(
        by_owner.astype(bf16), jnp.where(before, 1.0, 0.0).astype(bf16), preferred_element_type=f32
    )
    position = jnp.sum(by_owner * earlier, axis=0, keepdims=True)
    target = step.astype(f32) * part_cap + position
    for part in range(1, PARTS):
        target = target + jnp.where(position >= part * part_cap, 1.0, 0.0) * (
            part_slots - part_cap
        )
    slot_at = lax.broadcasted_iota(jnp.int32, (slots, rows), 0).astype(f32)
    route = jnp.where(slot_at == target, 1.0, 0.0)
    gather[...] = jnp.transpose(route).astype(bf16)
    route = route.astype(bf16)
    label = lax.broadcasted_iota(jnp.int32, (LANES, rows), 0) == local
    label = jnp.where(label, 1.0, 0.0).astype(bf16)
    labels = lax.dot_general(
        route, label, (((1,), (1,)), ((), ())), preferred_element_type=f32
    ).astype(bf16)
    for part in range(PARTS):
        for d in range(owners):
            into = label_out if d else label_in
            first = part * part_slots + d * part_cap
            into[d, part] = labels[first : first + part_cap]

    pl.semaphore_wait(barrier, peers - 1 + owners - 1)

    def label_copy(d):
        return pltpu.make_async_remote_copy(
            src_ref=label_out.at[d],
            dst_ref=label_in.at[d],
            send_sem=label_send.at[d],
            recv_sem=label_recv.at[d],
            device_id={"replica": lax.rem(replica + d, owners)},
            device_id_type=MESH,
        )

    def route_copy(part, d):
        return pltpu.make_async_remote_copy(
            src_ref=route_out.at[part, d],
            dst_ref=route_in.at[part, d],
            send_sem=route_send.at[part, d],
            recv_sem=route_recv.at[part, d],
            device_id={"replica": lax.rem(replica + d, owners)},
            device_id_type=MESH,
        )

    def delta_copy(part, d):
        return pltpu.make_async_remote_copy(
            src_ref=delta_out.at[part, d],
            dst_ref=delta_in.at[part, d],
            send_sem=delta_send.at[part, d],
            recv_sem=delta_recv.at[part, d],
            device_id={"replica": lax.rem(replica - d + owners, owners)},
            device_id_type=MESH,
        )

    def rank_copy(part, e):
        return pltpu.make_async_remote_copy(
            src_ref=rank_out.at[part],
            dst_ref=rank_in.at[part, e],
            send_sem=rank_send.at[part, e],
            recv_sem=rank_recv.at[part, e],
            device_id=tensor_peer(e),
            device_id_type=MESH,
        )

    def pair_copy(i):
        return pltpu.make_async_remote_copy(
            src_ref=pair_out.at[i],
            dst_ref=pair_in.at[i],
            send_sem=pair_send.at[i],
            recv_sem=pair_recv.at[i],
            device_id={"sub": 1 - sub},
            device_id_type=MESH,
        )

    def cross_copy(i):
        return pltpu.make_async_remote_copy(
            src_ref=cross_out.at[i],
            dst_ref=cross_in.at[i],
            send_sem=cross_send.at[i],
            recv_sem=cross_recv.at[i],
            device_id={"tensor": lax.rem(tensor + 1 + i // chunks, tensors)},
            device_id_type=MESH,
        )

    for d in range(1, owners):
        label_copy(d).start()

    for copy in now_copies:
        copy.wait()

    def attend_rows(i, carry):
        for copy in cache_copies(i):
            copy.wait()
        attend_block(
            i * block,
            block,
            length_ref,
            query_ref,
            key_now_ref,
            value_now_ref,
            key_ref,
            value_ref,
            attended_ref,
        )
        return carry

    lax.fori_loop(0, rows // block, attend_rows, 0)
    for part in range(PARTS):
        routed = jnp.dot(
            route[part * part_slots : (part + 1) * part_slots],
            attended_ref[...],
            preferred_element_type=f32,
        ).astype(bf16)
        for d in reversed(range(owners)):
            into = route_out if d else route_in
            into[part, d] = routed[d * part_cap : (d + 1) * part_cap]
            if d:
                route_copy(part, d).start()

    def product(slot):
        return jnp.dot(attended_ref[...], panel[slot], preferred_element_type=f32)

    def far_pair(i, carry):
        far_panel(i, False).wait()
        pair_out[i] = product(i).astype(bf16)
        pair_copy(i).start()
        return carry

    def far_mine(i, carry):
        far_panel(i, True).wait()
        mine = product(far + i)
        pair_copy(i).wait_recv()
        cross_out[i] = (mine + pair_in[i].astype(f32)).astype(bf16)
        return carry

    def far_send(i, carry):
        cross_copy(i).start()
        return carry

    def far_both(i, carry):
        return far_send(i, far_mine(i, carry))

    def near_pair(c, carry):
        near_panel(c, False).wait()
        pair_out[far + c] = product(2 * far + c).astype(bf16)
        pair_copy(far + c).start()
        return carry

    def near_mine(c, carry):
        near_panel(c, True).wait()
        base[c] = product(2 * far + chunks + c)
        return carry

    spread = lax.broadcasted_iota(jnp.int32, (LANES, wide), 0) == (
        lax.broadcasted_iota(jnp.int32, (LANES, wide), 1) // rank
    )
    spread = jnp.where(spread, 1.0, 0.0).astype(bf16)
    repeat = lax.broadcasted_iota(jnp.int32, (rank, wide), 0) == lax.rem(
        lax.broadcasted_iota(jnp.int32, (rank, wide), 1), rank
    )
    repeat = jnp.where(repeat, 1.0, 0.0).astype(bf16)

    def shrink(part):
        for d in reversed(range(1, owners)):
            route_copy(part, d).wait_recv()
        arrived = route_in[part].reshape(part_slots, feats)
        marks = label_in[:, part].reshape(part_slots, LANES)
        mask = jnp.dot(marks, spread, preferred_element_type=f32)
        product = lax.dot_general(
            arrived, down_ref[...], (((1,), (1,)), ((), ())), preferred_element_type=f32
        )
        product = jnp.where(mask > 0.5, product, 0.0)
        shrunk = product[:, :rank]
        for a in range(1, adp_local):
            shrunk = shrunk + product[:, a * rank : (a + 1) * rank]
        rank_out[part] = shrunk.astype(bf16)
        for e in range(1, peers):
            rank_copy(part, e).start()
        return shrunk, mask

    def expand(part, shrunk, mask):
        for e in range(1, peers):
            rank_copy(part, e).wait_recv()
            shrunk = shrunk + rank_in[part, e].astype(f32)
        held = jnp.dot(shrunk.astype(bf16), repeat, preferred_element_type=f32)
        held = jnp.where(mask > 0.5, held, 0.0).astype(bf16)
        delta = jnp.dot(held, up_ref[...], preferred_element_type=f32).astype(bf16)
        for d in reversed(range(owners)):
            into = delta_out if d else delta_in
            into[part, d] = delta[d * part_cap : (d + 1) * part_cap]
            if d:
                delta_copy(part, d).start()

    first, second = far // 4, far // 2
    lax.fori_loop(0, far, far_pair, 0)
    lax.fori_loop(0, first, far_both, 0)
    lax.fori_loop(first, far, far_mine, 0)
    for copy in weight_copies:
        copy.wait()
    for d in range(1, owners):
        label_copy(d).wait_recv()
    early = shrink(0)
    lax.fori_loop(0, chunks, near_pair, 0)
    expand(0, *early)
    lax.fori_loop(first, second, far_send, 0)
    late = shrink(1)
    lax.fori_loop(0, chunks, near_mine, 0)
    expand(1, *late)
    lax.fori_loop(second, far, far_send, 0)

    def near_add(c, carry):
        pair_copy(far + c).wait_recv()
        base[c] = base[c] + pair_in[far + c].astype(f32)
        return carry

    def far_add(i, carry):
        cross_copy(i).wait_recv()
        c = lax.rem(i, chunks)
        base[c] = base[c] + cross_in[i].astype(f32)
        return carry

    lax.fori_loop(0, chunks, near_add, 0)
    lax.fori_loop(0, far, far_add, 0)
    for part in range(PARTS):
        for d in range(1, owners):
            delta_copy(part, d).wait_recv()
        for c in range(chunks):
            at = slice(c * chunk, (c + 1) * chunk)
            total = base[c] + jnp.dot(
                gather[:, part * part_slots : (part + 1) * part_slots],
                delta_in[part, :, :, at].reshape(part_slots, chunk),
                preferred_element_type=f32,
            )
            if part < PARTS - 1:
                base[c] = total
            else:
                out_ref[:, at] = total.astype(bf16)

    for d in range(1, owners):
        label_copy(d).wait_send()
        for part in range(PARTS):
            route_copy(part, d).wait_send()
            delta_copy(part, d).wait_send()
    for e in range(1, peers):
        for part in range(PARTS):
            rank_copy(part, e).wait_send()

    def pair_sent(i, carry):
        pair_copy(i).wait_send()
        return carry

    def cross_sent(i, carry):
        cross_copy(i).wait_send()
        return carry

    lax.fori_loop(0, far + chunks, pair_sent, 0)
    lax.fori_loop(0, far, cross_sent, 0)


def on_device(
    queries,
    incoming_keys,
    incoming_values,
    cached_key_rows,
    cached_value_rows,
    cache_length,
    adapter_of_row,
    adapter_slot_table,
    output_projection,
    adapter_down_weights,
    adapter_up_weights,
):
    rows, feats = queries.shape
    context = cached_key_rows.shape[1]
    adp_local, _, rank = adapter_down_weights.shape
    columns = adapter_up_weights.shape[2]
    tensors = lax.axis_size("tensor")
    owners = lax.axis_size("replica")
    peers = tensors * lax.axis_size("sub")
    chunk = min(512, columns)
    chunks = columns // chunk
    far = (tensors - 1) * chunks
    bf16 = jnp.bfloat16
    vmem = pl.BlockSpec(memory_space=pltpu.VMEM)
    smem = pl.BlockSpec(memory_space=pltpu.SMEM)
    hbm = pl.BlockSpec(memory_space=pl.ANY)
    part_cap = CAP // PARTS
    dma = pltpu.SemaphoreType.DMA
    return pl.pallas_call(
        functools.partial(project_kernel, tensors, owners),
        out_shape=jax.ShapeDtypeStruct((rows, columns), bf16),
        in_specs=[smem, smem, vmem, vmem, hbm, hbm, hbm, hbm, hbm, hbm, hbm],
        out_specs=vmem,
        scratch_shapes=[
            pltpu.VMEM((rows, HEAD_WIDTH), bf16),
            pltpu.VMEM((rows, HEAD_WIDTH), bf16),
            pltpu.VMEM((rows, context, HEAD_WIDTH), bf16),
            pltpu.VMEM((rows, context, HEAD_WIDTH), bf16),
            pltpu.VMEM((adp_local * rank, feats), bf16),
            pltpu.VMEM((adp_local * rank, columns), bf16),
            pltpu.VMEM((rows, feats), bf16),
            pltpu.VMEM((peers * chunks, feats, chunk), bf16),
            pltpu.VMEM((far + chunks, rows, chunk), bf16),
            pltpu.VMEM((far + chunks, rows, chunk), bf16),
            pltpu.VMEM((far, rows, chunk), bf16),
            pltpu.VMEM((far, rows, chunk), bf16),
            pltpu.VMEM((chunks, rows, chunk), jnp.float32),
            pltpu.VMEM((PARTS, owners, part_cap, feats), bf16),
            pltpu.VMEM((PARTS, owners, part_cap, feats), bf16),
            pltpu.VMEM((owners, PARTS, part_cap, LANES), bf16),
            pltpu.VMEM((owners, PARTS, part_cap, LANES), bf16),
            pltpu.VMEM((PARTS, owners * part_cap, rank), bf16),
            pltpu.VMEM((PARTS, peers, owners * part_cap, rank), bf16),
            pltpu.VMEM((PARTS, owners, part_cap, columns), bf16),
            pltpu.VMEM((PARTS, owners, part_cap, columns), bf16),
            pltpu.VMEM((rows, owners * CAP), bf16),
            dma((2 * rows // min(64, rows),)),
            dma((4,)),
            dma((peers * chunks,)),
            dma((far + chunks,)),
            dma((far + chunks,)),
            dma((far,)),
            dma((far,)),
            dma((PARTS, owners)),
            dma((PARTS, owners)),
            dma((owners,)),
            dma((owners,)),
            dma((PARTS, peers)),
            dma((PARTS, peers)),
            dma((PARTS, owners)),
            dma((PARTS, owners)),
        ],
        compiler_params=pltpu.CompilerParams(
            collective_id=0, has_side_effects=True, vmem_limit_bytes=52 * 1024 * 1024
        ),
        name="project",
    )(
        adapter_slot_table,
        cache_length,
        adapter_of_row.reshape(1, rows),
        queries,
        incoming_keys,
        incoming_values,
        cached_key_rows,
        cached_value_rows,
        output_projection,
        jnp.swapaxes(adapter_down_weights, 1, 2).reshape(adp_local * rank, feats),
        adapter_up_weights.reshape(adp_local * rank, columns),
    )


def solution(mesh):
    return jax.shard_map(
        on_device,
        mesh=mesh,
        in_specs=(
            P(("group", "replica"), ("tensor", "sub")),
            P(("group", "replica"), "tensor"),
            P(("group", "replica"), "tensor"),
            P(("group", "replica"), None, "tensor"),
            P(("group", "replica"), None, "tensor"),
            P(("group", "replica")),
            P(("group", "replica")),
            P("group"),
            P(("tensor", "sub"), None),
            P("replica", ("tensor", "sub"), None),
            P("replica", None, ("tensor", "sub")),
        ),
        out_specs=P(("group", "replica"), ("tensor", "sub")),
        check_vma=False,
    )
```

```python
import functools

import jax
import jax.numpy as jnp
from jax import lax
from jax.experimental import pallas as pl
from jax.experimental.pallas import tpu as pltpu
from jax.sharding import PartitionSpec as P

QUERY_HEADS = 32
KV_HEADS = 4
HEAD_WIDTH = 128
CAP = 64
LANES = 128
PARTS = 2
MESH = pl.DeviceIdType.MESH


def attend_block(
    first_row, block, length_ref, query_ref, key_now_ref, value_now_ref, key_ref, value_ref, out_ref
):
    heads = query_ref.shape[1] // HEAD_WIDTH
    context = key_ref.shape[1]
    rows = LANES // heads
    copies = LANES // context
    lane = lax.broadcasted_iota(jnp.int32, (1, LANES), 1)
    lane_row = lax.rem(lane, rows)
    row_masks = [lane_row == r for r in range(rows)]
    place = lax.broadcasted_iota(jnp.int32, (context, LANES), 0)
    side = lax.broadcasted_iota(jnp.int32, (LANES, LANES), 0)
    across = lax.broadcasted_iota(jnp.int32, (LANES, LANES), 1)
    fresh_mask = side == lax.rem(across, rows)
    offset = lax.rem(side, rows) - across // context
    score_scale = HEAD_WIDTH ** (-0.5)
    contract_last = (((1,), (1,)), ((), ()))
    for group in range(block // rows):
        at = pl.ds(pl.multiple_of(first_row + group * rows, rows), rows)
        stacked = jnp.concatenate(
            [query_ref[at, h * HEAD_WIDTH : (h + 1) * HEAD_WIDTH] for h in range(heads)], axis=0
        )
        keys = key_ref[at].reshape(rows * context, HEAD_WIDTH)
        wide = lax.dot_general(
            keys, stacked, contract_last, preferred_element_type=jnp.float32
        ).reshape(rows, context, LANES)
        lengths = jnp.zeros((1, LANES), jnp.int32)
        scores = wide[0]
        for r in range(rows):
            lengths = jnp.where(row_masks[r], length_ref[first_row + group * rows + r], lengths)
            scores = jnp.where(row_masks[r], wide[r], scores)
        now = lax.dot_general(
            key_now_ref[at], stacked, contract_last, preferred_element_type=jnp.float32
        )
        fresh = jnp.sum(jnp.where(fresh_mask[:rows], now, 0.0), axis=0, keepdims=True)
        fresh = fresh * score_scale
        scores = jnp.where(place < lengths, scores * score_scale, -1e30)
        highest = jnp.maximum(jnp.max(scores, axis=0, keepdims=True), fresh)
        weights = jnp.exp(scores - highest)
        fresh_weight = jnp.exp(fresh - highest)
        total = jnp.sum(weights, axis=0, keepdims=True) + fresh_weight
        turned = jnp.transpose(jnp.concatenate([weights] * copies, axis=0))
        extra = jnp.where(side < rows, jnp.where(fresh_mask, fresh_weight, 0.0), total)
        extra = jnp.transpose(extra)
        spread = jnp.concatenate(
            [
                jnp.where(offset == t * copies, turned, 0.0).astype(jnp.bfloat16)
                for t in range(rows // copies)
            ],
            axis=1,
        )
        values = value_ref[at].reshape(rows * context, HEAD_WIDTH)
        mixed = jnp.dot(spread, values, preferred_element_type=jnp.float32)
        mixed = mixed + jnp.dot(
            extra[:, :rows].astype(jnp.bfloat16),
            value_now_ref[at],
            preferred_element_type=jnp.float32,
        )
        attended = (mixed / extra[:, rows : rows + 1]).astype(jnp.bfloat16)
        for h in range(heads):
            out_ref[at, h * HEAD_WIDTH : (h + 1) * HEAD_WIDTH] = attended[h * rows : (h + 1) * rows]


def project_kernel(
    tensors,
    owners,
    table_ref,
    length_ref,
    adapter_ref,
    query_ref,
    fresh_key_ref,
    fresh_value_ref,
    stored_key_ref,
    stored_value_ref,
    projection_ref,
    stored_down_ref,
    stored_up_ref,
    out_ref,
    key_now_ref,
    value_now_ref,
    key_ref,
    value_ref,
    down_ref,
    up_ref,
    attended_ref,
    panel,
    pair_out,
    pair_in,
    cross_out,
    cross_in,
    base,
    route_out,
    route_in,
    label_out,
    label_in,
    rank_out,
    rank_in,
    delta_out,
    delta_in,
    gather,
    cache_sem,
    weight_sem,
    panel_sem,
    pair_send,
    pair_recv,
    cross_send,
    cross_recv,
    route_send,
    route_recv,
    label_send,
    label_recv,
    rank_send,
    rank_recv,
    delta_send,
    delta_recv,
):
    bf16, f32 = jnp.bfloat16, jnp.float32
    replica = lax.axis_index("replica")
    tensor = lax.axis_index("tensor")
    sub = lax.axis_index("sub")
    rows, feats = attended_ref.shape
    block = min(64, rows)
    heads = feats // HEAD_WIDTH
    head_at = pl.ds(
        pl.multiple_of(sub * heads // (QUERY_HEADS // KV_HEADS) * HEAD_WIDTH, HEAD_WIDTH), HEAD_WIDTH
    )
    chunk = panel.shape[2]
    columns = out_ref.shape[1]
    chunks = columns // chunk
    peers = tensors * 2
    far = (tensors - 1) * chunks
    rank = rank_out.shape[2]
    wide = down_ref.shape[0]
    adp_local = wide // rank
    part_cap = CAP // PARTS
    part_slots = owners * part_cap
    place = tensor * 2 + sub

    def tensor_peer(e):
        other = lax.rem(place + e, peers)
        return {"tensor": other // 2, "sub": lax.rem(other, 2)}

    barrier = pltpu.get_barrier_semaphore()
    for e in range(1, peers):
        pl.semaphore_signal(barrier, inc=1, device_id=tensor_peer(e), device_id_type=MESH)
    for d in range(1, owners):
        pl.semaphore_signal(
            barrier, inc=1, device_id={"replica": lax.rem(replica + d, owners)}, device_id_type=MESH
        )

    def panel_copy(slot, other_tensor, other_sub, c):
        start = pl.multiple_of((other_tensor * 2 + other_sub) * columns + c * chunk, chunk)
        return pltpu.make_async_copy(
            projection_ref.at[:, pl.ds(start, chunk)], panel.at[slot], panel_sem.at[slot]
        )

    def far_panel(i, mine):
        other = lax.rem(tensor + 1 + i // chunks, tensors)
        side = sub if mine else 1 - sub
        return panel_copy(i + (far if mine else 0), other, side, lax.rem(i, chunks))

    def near_panel(c, mine):
        side = sub if mine else 1 - sub
        return panel_copy(2 * far + (chunks if mine else 0) + c, tensor, side, c)

    def cache_copies(i):
        at = pl.ds(pl.multiple_of(i * block, block), block)
        return [
            pltpu.make_async_copy(
                stored.at[at, :, head_at], kept.at[at], cache_sem.at[2 * i + which]
            )
            for which, (stored, kept) in enumerate(
                [(stored_key_ref, key_ref), (stored_value_ref, value_ref)]
            )
        ]

    weight_copies = [
        pltpu.make_async_copy(stored_down_ref, down_ref, weight_sem.at[0]),
        pltpu.make_async_copy(stored_up_ref, up_ref, weight_sem.at[1]),
    ]
    now_copies = [
        pltpu.make_async_copy(fresh_key_ref.at[:, head_at], key_now_ref, weight_sem.at[2]),
        pltpu.make_async_copy(fresh_value_ref.at[:, head_at], value_now_ref, weight_sem.at[3]),
    ]
    for copy in now_copies:
        copy.start()
    for i in range(rows // block):
        for copy in cache_copies(i):
            copy.start()
    for i in range(far):
        far_panel(i, False).start()
    for i in range(far):
        far_panel(i, True).start()
    for c in range(chunks):
        near_panel(c, False).start()
    for c in range(chunks):
        near_panel(c, True).start()
    for copy in weight_copies:
        copy.start()

    slots = owners * CAP
    adapters = adapter_ref[...]
    stored = jnp.zeros_like(adapters)
    for a in range(table_ref.shape[0]):
        stored = jnp.where(adapters == a, table_ref[a], stored)
    owner = stored // adp_local
    local = stored - owner * adp_local
    step = lax.rem(owner - replica + owners, owners)
    by_owner = lax.broadcasted_iota(jnp.int32, (max(owners, 8), rows), 0) == step
    before = lax.broadcasted_iota(jnp.int32, (rows, rows), 0) < lax.broadcasted_iota(
        jnp.int32, (rows, rows), 1
    )
    by_owner = jnp.where(by_owner, 1.0, 0.0)
    earlier = jnp.dot(
        by_owner.astype(bf16), jnp.where(before, 1.0, 0.0).astype(bf16), preferred_element_type=f32
    )
    position = jnp.sum(by_owner * earlier, axis=0, keepdims=True)
    target = step.astype(f32) * part_cap + position
    for part in range(1, PARTS):
        target = target + jnp.where(position >= part * part_cap, 1.0, 0.0) * (
            part_slots - part_cap
        )
    slot_at = lax.broadcasted_iota(jnp.int32, (slots, rows), 0).astype(f32)
    route = jnp.where(slot_at == target, 1.0, 0.0)
    gather[...] = jnp.transpose(route).astype(bf16)
    route = route.astype(bf16)
    label = lax.broadcasted_iota(jnp.int32, (LANES, rows), 0) == local
    label = jnp.where(label, 1.0, 0.0).astype(bf16)
    labels = lax.dot_general(
        route, label, (((1,), (1,)), ((), ())), preferred_element_type=f32
    ).astype(bf16)
    for part in range(PARTS):
        for d in range(owners):
            into = label_out if d else label_in
            first = part * part_slots + d * part_cap
            into[d, part] = labels[first : first + part_cap]

    pl.semaphore_wait(barrier, peers - 1 + owners - 1)

    def label_copy(d):
        return pltpu.make_async_remote_copy(
            src_ref=label_out.at[d],
            dst_ref=label_in.at[d],
            send_sem=label_send.at[d],
            recv_sem=label_recv.at[d],
            device_id={"replica": lax.rem(replica + d, owners)},
            device_id_type=MESH,
        )

    def route_copy(part, d):
        return pltpu.make_async_remote_copy(
            src_ref=route_out.at[part, d],
            dst_ref=route_in.at[part, d],
            send_sem=route_send.at[part, d],
            recv_sem=route_recv.at[part, d],
            device_id={"replica": lax.rem(replica + d, owners)},
            device_id_type=MESH,
        )

    def delta_copy(part, d):
        return pltpu.make_async_remote_copy(
            src_ref=delta_out.at[part, d],
            dst_ref=delta_in.at[part, d],
            send_sem=delta_send.at[part, d],
            recv_sem=delta_recv.at[part, d],
            device_id={"replica": lax.rem(replica - d + owners, owners)},
            device_id_type=MESH,
        )

    def rank_copy(part, e):
        return pltpu.make_async_remote_copy(
            src_ref=rank_out.at[part],
            dst_ref=rank_in.at[part, e],
            send_sem=rank_send.at[part, e],
            recv_sem=rank_recv.at[part, e],
            device_id=tensor_peer(e),
            device_id_type=MESH,
        )

    def pair_copy(i):
        return pltpu.make_async_remote_copy(
            src_ref=pair_out.at[i],
            dst_ref=pair_in.at[i],
            send_sem=pair_send.at[i],
            recv_sem=pair_recv.at[i],
            device_id={"sub": 1 - sub},
            device_id_type=MESH,
        )

    def cross_copy(i):
        return pltpu.make_async_remote_copy(
            src_ref=cross_out.at[i],
            dst_ref=cross_in.at[i],
            send_sem=cross_send.at[i],
            recv_sem=cross_recv.at[i],
            device_id={"tensor": lax.rem(tensor + 1 + i // chunks, tensors)},
            device_id_type=MESH,
        )

    for d in range(1, owners):
        label_copy(d).start()

    for copy in now_copies:
        copy.wait()

    def attend_rows(i, carry):
        for copy in cache_copies(i):
            copy.wait()
        attend_block(
            i * block,
            block,
            length_ref,
            query_ref,
            key_now_ref,
            value_now_ref,
            key_ref,
            value_ref,
            attended_ref,
        )
        return carry

    lax.fori_loop(0, rows // block, attend_rows, 0)
    for part in range(PARTS):
        routed = jnp.dot(
            route[part * part_slots : (part + 1) * part_slots],
            attended_ref[...],
            preferred_element_type=f32,
        ).astype(bf16)
        for d in reversed(range(owners)):
            into = route_out if d else route_in
            into[part, d] = routed[d * part_cap : (d + 1) * part_cap]
            if d:
                route_copy(part, d).start()

    def product(slot):
        return jnp.dot(attended_ref[...], panel[slot], preferred_element_type=f32)

    def far_pair(i, carry):
        far_panel(i, False).wait()
        pair_out[i] = product(i).astype(bf16)
        pair_copy(i).start()
        return carry

    def far_mine(i, carry):
        far_panel(i, True).wait()
        mine = product(far + i)
        pair_copy(i).wait_recv()
        cross_out[i] = (mine + pair_in[i].astype(f32)).astype(bf16)
        return carry

    def far_send(i, carry):
        cross_copy(i).start()
        return carry

    def far_both(i, carry):
        return far_send(i, far_mine(i, carry))

    def near_pair(c, carry):
        near_panel(c, False).wait()
        pair_out[far + c] = product(2 * far + c).astype(bf16)
        pair_copy(far + c).start()
        return carry

    def near_mine(c, carry):
        near_panel(c, True).wait()
        base[c] = product(2 * far + chunks + c)
        return carry

    spread = lax.broadcasted_iota(jnp.int32, (LANES, wide), 0) == (
        lax.broadcasted_iota(jnp.int32, (LANES, wide), 1) // rank
    )
    spread = jnp.where(spread, 1.0, 0.0).astype(bf16)
    repeat = lax.broadcasted_iota(jnp.int32, (rank, wide), 0) == lax.rem(
        lax.broadcasted_iota(jnp.int32, (rank, wide), 1), rank
    )
    repeat = jnp.where(repeat, 1.0, 0.0).astype(bf16)

    def shrink(part):
        for d in reversed(range(1, owners)):
            route_copy(part, d).wait_recv()
        arrived = route_in[part].reshape(part_slots, feats)
        marks = label_in[:, part].reshape(part_slots, LANES)
        mask = jnp.dot(marks, spread, preferred_element_type=f32)
        product = lax.dot_general(
            arrived, down_ref[...], (((1,), (1,)), ((), ())), preferred_element_type=f32
        )
        product = jnp.where(mask > 0.5, product, 0.0)
        shrunk = product[:, :rank]
        for a in range(1, adp_local):
            shrunk = shrunk + product[:, a * rank : (a + 1) * rank]
        rank_out[part] = shrunk.astype(bf16)
        for e in range(1, peers):
            rank_copy(part, e).start()
        return shrunk, mask

    def expand(part, shrunk, mask):
        for e in range(1, peers):
            rank_copy(part, e).wait_recv()
            shrunk = shrunk + rank_in[part, e].astype(f32)
        held = jnp.dot(shrunk.astype(bf16), repeat, preferred_element_type=f32)
        held = jnp.where(mask > 0.5, held, 0.0).astype(bf16)
        delta = jnp.dot(held, up_ref[...], preferred_element_type=f32).astype(bf16)
        for d in reversed(range(owners)):
            into = delta_out if d else delta_in
            into[part, d] = delta[d * part_cap : (d + 1) * part_cap]
            if d:
                delta_copy(part, d).start()

    first = far // 4
    lax.fori_loop(0, far, far_pair, 0)
    lax.fori_loop(0, first, far_both, 0)
    for copy in weight_copies:
        copy.wait()
    for d in range(1, owners):
        label_copy(d).wait_recv()
    early = shrink(0)
    lax.fori_loop(first, far, far_mine, 0)
    late = shrink(1)
    lax.fori_loop(first, far, far_send, 0)
    expand(0, *early)
    expand(1, *late)
    lax.fori_loop(0, chunks, near_pair, 0)
    lax.fori_loop(0, chunks, near_mine, 0)

    def near_add(c, carry):
        pair_copy(far + c).wait_recv()
        base[c] = base[c] + pair_in[far + c].astype(f32)
        return carry

    def far_add(i, carry):
        cross_copy(i).wait_recv()
        c = lax.rem(i, chunks)
        base[c] = base[c] + cross_in[i].astype(f32)
        return carry

    lax.fori_loop(0, chunks, near_add, 0)
    lax.fori_loop(0, far, far_add, 0)
    for part in range(PARTS):
        for d in range(1, owners):
            delta_copy(part, d).wait_recv()
        for c in range(chunks):
            at = slice(c * chunk, (c + 1) * chunk)
            total = base[c] + jnp.dot(
                gather[:, part * part_slots : (part + 1) * part_slots],
                delta_in[part, :, :, at].reshape(part_slots, chunk),
                preferred_element_type=f32,
            )
            if part < PARTS - 1:
                base[c] = total
            else:
                out_ref[:, at] = total.astype(bf16)

    for d in range(1, owners):
        label_copy(d).wait_send()
        for part in range(PARTS):
            route_copy(part, d).wait_send()
            delta_copy(part, d).wait_send()
    for e in range(1, peers):
        for part in range(PARTS):
            rank_copy(part, e).wait_send()

    def pair_sent(i, carry):
        pair_copy(i).wait_send()
        return carry

    def cross_sent(i, carry):
        cross_copy(i).wait_send()
        return carry

    lax.fori_loop(0, far + chunks, pair_sent, 0)
    lax.fori_loop(0, far, cross_sent, 0)


def on_device(
    queries,
    incoming_keys,
    incoming_values,
    cached_key_rows,
    cached_value_rows,
    cache_length,
    adapter_of_row,
    adapter_slot_table,
    output_projection,
    adapter_down_weights,
    adapter_up_weights,
):
    rows, feats = queries.shape
    context = cached_key_rows.shape[1]
    adp_local, _, rank = adapter_down_weights.shape
    columns = adapter_up_weights.shape[2]
    tensors = lax.axis_size("tensor")
    owners = lax.axis_size("replica")
    peers = tensors * lax.axis_size("sub")
    chunk = min(512, columns)
    chunks = columns // chunk
    far = (tensors - 1) * chunks
    bf16 = jnp.bfloat16
    vmem = pl.BlockSpec(memory_space=pltpu.VMEM)
    smem = pl.BlockSpec(memory_space=pltpu.SMEM)
    hbm = pl.BlockSpec(memory_space=pl.ANY)
    part_cap = CAP // PARTS
    dma = pltpu.SemaphoreType.DMA
    return pl.pallas_call(
        functools.partial(project_kernel, tensors, owners),
        out_shape=jax.ShapeDtypeStruct((rows, columns), bf16),
        in_specs=[smem, smem, vmem, vmem, hbm, hbm, hbm, hbm, hbm, hbm, hbm],
        out_specs=vmem,
        scratch_shapes=[
            pltpu.VMEM((rows, HEAD_WIDTH), bf16),
            pltpu.VMEM((rows, HEAD_WIDTH), bf16),
            pltpu.VMEM((rows, context, HEAD_WIDTH), bf16),
            pltpu.VMEM((rows, context, HEAD_WIDTH), bf16),
            pltpu.VMEM((adp_local * rank, feats), bf16),
            pltpu.VMEM((adp_local * rank, columns), bf16),
            pltpu.VMEM((rows, feats), bf16),
            pltpu.VMEM((peers * chunks, feats, chunk), bf16),
            pltpu.VMEM((far + chunks, rows, chunk), bf16),
            pltpu.VMEM((far + chunks, rows, chunk), bf16),
            pltpu.VMEM((far, rows, chunk), bf16),
            pltpu.VMEM((far, rows, chunk), bf16),
            pltpu.VMEM((chunks, rows, chunk), jnp.float32),
            pltpu.VMEM((PARTS, owners, part_cap, feats), bf16),
            pltpu.VMEM((PARTS, owners, part_cap, feats), bf16),
            pltpu.VMEM((owners, PARTS, part_cap, LANES), bf16),
            pltpu.VMEM((owners, PARTS, part_cap, LANES), bf16),
            pltpu.VMEM((PARTS, owners * part_cap, rank), bf16),
            pltpu.VMEM((PARTS, peers, owners * part_cap, rank), bf16),
            pltpu.VMEM((PARTS, owners, part_cap, columns), bf16),
            pltpu.VMEM((PARTS, owners, part_cap, columns), bf16),
            pltpu.VMEM((rows, owners * CAP), bf16),
            dma((2 * rows // min(64, rows),)),
            dma((4,)),
            dma((peers * chunks,)),
            dma((far + chunks,)),
            dma((far + chunks,)),
            dma((far,)),
            dma((far,)),
            dma((PARTS, owners)),
            dma((PARTS, owners)),
            dma((owners,)),
            dma((owners,)),
            dma((PARTS, peers)),
            dma((PARTS, peers)),
            dma((PARTS, owners)),
            dma((PARTS, owners)),
        ],
        compiler_params=pltpu.CompilerParams(
            collective_id=0, has_side_effects=True, vmem_limit_bytes=63 * 1024 * 1024
        ),
        name="project",
    )(
        adapter_slot_table,
        cache_length,
        adapter_of_row.reshape(1, rows),
        queries,
        incoming_keys,
        incoming_values,
        cached_key_rows,
        cached_value_rows,
        output_projection,
        jnp.swapaxes(adapter_down_weights, 1, 2).reshape(adp_local * rank, feats),
        adapter_up_weights.reshape(adp_local * rank, columns),
    )


def solution(mesh):
    return jax.shard_map(
        on_device,
        mesh=mesh,
        in_specs=(
            P(("group", "replica"), ("tensor", "sub")),
            P(("group", "replica"), "tensor"),
            P(("group", "replica"), "tensor"),
            P(("group", "replica"), None, "tensor"),
            P(("group", "replica"), None, "tensor"),
            P(("group", "replica")),
            P(("group", "replica")),
            P("group"),
            P(("tensor", "sub"), None),
            P("replica", ("tensor", "sub"), None),
            P("replica", None, ("tensor", "sub")),
        ),
        out_specs=P(("group", "replica"), ("tensor", "sub")),
        check_vma=False,
    )
```
